512 devices in a mesh: row: 32 (over z_lo, x, core), col: 16 (over z_hi, y).
Axes of the slice: x: 4, y: 4, z: 16 (z_hi: 4, z_lo: 4; z = z_hi * 4 + z_lo), core: 2. Of those that a mesh axis runs over, the one named last changes fastest.
Arguments:
- acts_in: bfloat16 [1024, 8192], P('col', 'row'), may hold values from -72 to 72, as said below
- grad_hidden: bfloat16 [1024, 32768], P('row', 'col'), may hold values from -1.2 to 1.2, as said below
- acts_hidden: bfloat16 [1024, 32768], P('col', 'row'), may hold values from -72 to 72, as said below
- grad_out: bfloat16 [1024, 8192], P('row', 'col'), may hold values from -1.2 to 1.2, as said below
- row_state_up: float32 [8192], P('row'), may hold values from 0.01 to 1
- col_state_up: float32 [32768], P('col'), may hold values from 0.01 to 1
- row_state_down: float32 [32768], P('row'), may hold values from 0.01 to 1
- col_state_down: float32 [8192], P('col'), may hold values from 0.01 to 1
Outputs:
- update_up: bfloat16 [8192, 32768], P('row', 'col')
- row_new_up: float32 [8192], P('row')
- col_new_up: float32 [32768], P('col')
- update_down: bfloat16 [32768, 8192], P('row', 'col')
- row_new_down: float32 [32768], P('row')
- col_new_down: float32 [8192], P('col')
The draws below stay inside these ranges and needn't reach their ends.
Inputs may be any that keep to these rules, and one draw needn't show every extreme that they name: `acts_in`: real-valued entries. `grad_hidden`: real-valued entries. `acts_hidden`: real-valued entries. `grad_out`: real-valued entries.
All inputs are finite; a program needn't handle non-finite values.
Results may differ from the reference program's by a relative error of at most 0.001.
Values may be sent and summed in bfloat16 or wider, within the bound.
A program may use at most 64 MiB of HBM per device.

```python
import math
import jax
import jax.numpy as jnp
from jax import lax

D = 8192
FF = 32768
TOKENS = 1024


def spread_scales(key, rows, cols):
    key_row, key_col = jax.random.split(key)
    row_scale = jnp.exp(jax.random.uniform(key_row, (rows, 1), jnp.float32, -1.15, 1.15))
    ramp = 0.6 + 1.2 * jnp.arange(cols, dtype=jnp.float32) / cols
    col_scale = jnp.exp(jax.random.uniform(key_col, (1, cols), jnp.float32, -1.15, 1.15)) * ramp
    return row_scale * col_scale


def draw_acts_in(key, part):
    key = jax.random.fold_in(key, 11)
    key_base = jax.random.fold_in(key, 0)
    key_scale = jax.random.fold_in(key, 2)
    base = jax.random.truncated_normal(key_base, -4.0, 4.0, (TOKENS, D), jnp.float32)
    return (base * spread_scales(key_scale, TOKENS, D)).astype(jnp.bfloat16)


def draw_grad_hidden(key, part):
    key = jax.random.fold_in(key, 12)
    key_base = jax.random.fold_in(key, 0)
    key_scale = jax.random.fold_in(key, 2)
    base = jax.random.truncated_normal(key_base, -4.0, 4.0, (TOKENS, FF), jnp.float32)
    return (base * spread_scales(key_scale, TOKENS, FF) / 64.0).astype(jnp.bfloat16)


def draw_acts_hidden(key, part):
    key = jax.random.fold_in(key, 13)
    key_base = jax.random.fold_in(key, 0)
    key_scale = jax.random.fold_in(key, 2)
    base = jax.random.truncated_normal(key_base, -4.0, 4.0, (TOKENS, FF), jnp.float32)
    return (base * spread_scales(key_scale, TOKENS, FF)).astype(jnp.bfloat16)


def draw_grad_out(key, part):
    key = jax.random.fold_in(key, 14)
    key_base = jax.random.fold_in(key, 0)
    key_scale = jax.random.fold_in(key, 2)
    base = jax.random.truncated_normal(key_base, -4.0, 4.0, (TOKENS, D), jnp.float32)
    return (base * spread_scales(key_scale, TOKENS, D) / 64.0).astype(jnp.bfloat16)


def steps_of(key, extent, shards, smallest, high):
    gain = 1.0
    for axis_at, shards_of in shards:
        heights = jax.random.uniform(jax.random.fold_in(jax.random.fold_in(key, 6), axis_at), (shards_of,), jnp.float32, smallest / len(shards), high / len(shards))
        gain = gain * jnp.repeat(jnp.exp(heights), extent[axis_at] // shards_of).reshape((-1,) + (1,) * (len(extent) - 1 - axis_at))
    return gain


def setup_inputs(seed: int = 0) -> dict:
    seeds = jax.random.split(jax.random.key(seed), 9)
    return {
        "acts_in": draw_acts_in(jax.random.fold_in(seeds[8], 71), 0),
        "grad_hidden": draw_grad_hidden(jax.random.fold_in(seeds[8], 71), 0),
        "acts_hidden": draw_acts_hidden(jax.random.fold_in(seeds[8], 71), 0),
        "grad_out": draw_grad_out(jax.random.fold_in(seeds[8], 71), 0),
        "row_state_up": jnp.clip(jnp.exp(math.log(1.0) - 4.6051702 * jax.random.uniform(seeds[4], (D,), jnp.float32) ** steps_of(seeds[4], (D,), ((0, 32),), -0.2, 0.2)), 0.01, 1.0),
        "col_state_up": jnp.clip(jnp.exp(math.log(1.0) - 4.6051702 * jax.random.uniform(seeds[5], (FF,), jnp.float32) ** steps_of(seeds[5], (FF,), ((0, 16),), -0.2, 0.2)), 0.01, 1.0),
        "row_state_down": jnp.clip(jnp.exp(math.log(1.0) - 4.6051702 * jax.random.uniform(seeds[6], (FF,), jnp.float32) ** steps_of(seeds[6], (FF,), ((0, 32),), -0.2, 0.2)), 0.01, 1.0),
        "col_state_down": jnp.clip(jnp.exp(math.log(1.0) - 4.6051702 * jax.random.uniform(seeds[7], (D,), jnp.float32) ** steps_of(seeds[7], (D,), ((0, 16),), -0.2, 0.2)), 0.01, 1.0),
    }


DECAY = 1.0 - 10.0 ** (-0.8)
EPS_SQUARE = 1e-30
CLIP_FLOOR = 0.1

def factored_step(grad, row_state, col_state):
    square = grad * grad + EPS_SQUARE
    row_new = DECAY * row_state + (1.0 - DECAY) * (lax.optimization_barrier(jnp.sum(square, axis=1)) / grad.shape[1])
    col_new = DECAY * col_state + (1.0 - DECAY) * (lax.optimization_barrier(jnp.sum(square, axis=0)) / grad.shape[0])
    raw = grad / jnp.sqrt(row_new[:, None] * col_new[None, :])
    rms = jnp.sqrt(jnp.sum(raw * raw) / (grad.shape[0] * grad.shape[1]))
    update = (raw / jnp.maximum(CLIP_FLOOR, rms)).astype(jnp.bfloat16)
    return (update, row_new, col_new)

def reference(acts_in, grad_hidden, acts_hidden, grad_out, row_state_up, col_state_up, row_state_down, col_state_down):
    grad_up = jnp.dot(acts_in.T, grad_hidden, preferred_element_type=jnp.float32)
    update_up, row_new_up, col_new_up = factored_step(grad_up, row_state_up, col_state_up)
    grad_down = jnp.dot(acts_hidden.T, grad_out, preferred_element_type=jnp.float32)
    update_down, row_new_down, col_new_down = factored_step(grad_down, row_state_down, col_state_down)
    return (update_up, row_new_up, col_new_up, update_down, row_new_down, col_new_down)
```

```python
import functools

import jax
import jax.numpy as jnp
from jax import lax
from jax.experimental import pallas as pl
from jax.experimental.pallas import tpu as pltpu
from jax.sharding import PartitionSpec as P

D = 8192
FF = 32768
DECAY = 1.0 - 10.0 ** (-0.8)
EPS_SQUARE = 1e-30
CLIP_FLOOR = 0.1

NB = 16
ROWS = 32
COLS = 16
F32 = jnp.float32
BF16 = jnp.bfloat16
MESH = pl.DeviceIdType.MESH
NSEND = 112


def mod(a, n):
    return lax.rem(a + n, n)


def kernel(
    ai_in, h_in, ah_in, o_in, rsu_in, csu_in, rsd_in, csd_in,
    uu_out, rnu_out, cnu_out, ud_out, rnd_out, cnd_out,
    ai, ah, h, o, gu, gd, uu, ud, rbu, rbd,
    rstate, cstate, rnew, cnew, rpart, cpart, rbuf, cbuf, tpart, tbuf1, tpart2, tbuf2,
    ai_sem, ah_sem, h_sem, o_sem, hs_sem, os_sem, send_sem, loc_sem, out_sem,
    r_recv, c_recv, r_send, c_send, t1_recv, t1_send, t2_recv, t2_send,
):
    r = lax.axis_index("row")
    c = lax.axis_index("col")
    core = lax.rem(r, 2)
    x = lax.rem(r // 2, 4)
    p = r // 8
    y = lax.rem(c, 4)
    zh = c // 4
    s = 1 - 2 * core

    def row_at(zl_, x_, core_):
        return (zl_ * 8 + x_ * 2 + core_, c)

    def col_at(zh_, y_):
        return (r, zh_ * 4 + y_)

    xf, xb = mod(x + s, 4), mod(x - s, 4)
    yf, yb = mod(y + s, 4), mod(y - s, 4)
    zf, zb = mod(zh + s, 4), mod(zh - s, 4)
    x_f, x_b = row_at(p, xf, core), row_at(p, xb, core)
    y_f, y_b = col_at(zh, yf), col_at(zh, yb)
    z_f, z_b = col_at(zf, y), col_at(zb, y)
    l_f, l_b = row_at(mod(p + 1, 4), x, core), row_at(mod(p - 1, 4), x, core)
    sib = row_at(p, x, 1 - core)

    barrier = pltpu.get_barrier_semaphore()
    for dev in (x_f, x_b, y_f, y_b, z_f, z_b, l_f, l_b, sib):
        pl.semaphore_signal(barrier, inc=1, device_id=dev, device_id_type=MESH)
    pl.semaphore_wait(barrier, 9)

    sends = []
    nsend = [0]

    def send(src, dst, recv, like, dev, conds=()):
        k = nsend[0]
        nsend[0] += 1
        pltpu.make_async_remote_copy(src, dst, send_sem.at[k], recv, dev, MESH).start()
        sends.append((like, k, conds))

    def when(conds, f):
        if not conds:
            f()
        else:
            pl.when(conds[0])(lambda: when(conds[1:], f))

    def arrived(dst, recv, like=None):
        pltpu.make_async_remote_copy(dst, dst, send_sem.at[0], recv, sib, MESH).wait_recv()

    def hslot(b):
        return h.at[b, core], h_sem.at[b], lambda: h.at[0, 0]

    def oslot(b):
        return o.at[b, core], o_sem.at[b], lambda: o.at[0, 0]

    def aislot(b):
        return ai.at[b], ai_sem.at[b], lambda: ai.at[0]

    def ahslot(b):
        return ah.at[b], ah_sem.at[b], lambda: ah.at[0]

    not_last, not_first = p < 3, p > 0

    own_r, own_c = p * 4 + x, c
    ROWG = ((h_in, hslot), (o_in, oslot))

    def line_own():
        @pl.when(not_last)
        def _():
            for src, slot in ROWG:
                send(src, *slot(own_r), l_f, (not_last,))

        @pl.when(not_first)
        def _():
            for src, slot in ROWG:
                send(src, *slot(own_r), l_b, (not_first,))

    line_own()
    for dev in (z_f, z_b):
        send(ai_in, *aislot(own_c), dev)
    for src, slot in ROWG:
        for dev in (x_f, x_b):
            send(src, *slot(own_r), dev)
    for src, slot in ((ai_in, aislot), (ah_in, ahslot)):
        for dev in (y_f, y_b):
            send(src, *slot(own_c), dev)
    for dev in (z_f, z_b):
        send(ah_in, *ahslot(own_c), dev)

    local = [
        pltpu.make_async_copy(ai_in, ai.at[own_c], loc_sem.at[0]),
        pltpu.make_async_copy(ah_in, ah.at[own_c], loc_sem.at[1]),
        pltpu.make_async_copy(h_in, h.at[own_r, core], loc_sem.at[2]),
        pltpu.make_async_copy(o_in, o.at[own_r, core], loc_sem.at[3]),
        pltpu.make_async_copy(rsu_in, rstate.at[pl.ds(8, 2)], loc_sem.at[4]),
        pltpu.make_async_copy(rsd_in, rstate.at[pl.ds(0, 8)], loc_sem.at[5]),
        pltpu.make_async_copy(csu_in, cstate.at[pl.ds(0, 16)], loc_sem.at[6]),
        pltpu.make_async_copy(csd_in, cstate.at[pl.ds(16, 4)], loc_sem.at[7]),
    ]
    for copy in local:
        copy.start()

    def line(d):
        left, right = p >= d, p + d <= 3

        @pl.when(left)
        def _():
            b = (p - d) * 4 + x
            for _, slot in ROWG:
                arrived(*slot(b))
            if d < 3:
                @pl.when(not_last)
                def _():
                    for _, slot in ROWG:
                        send(slot(b)[0], *slot(b), l_f, (left, not_last))
            for _, slot in ROWG:
                for dev in (x_f, x_b):
                    send(slot(b)[0], *slot(b), dev, (left,))

        @pl.when(right)
        def _():
            b = (p + d) * 4 + x
            for _, slot in ROWG:
                arrived(*slot(b))
            if d < 3:
                @pl.when(not_first)
                def _():
                    for _, slot in ROWG:
                        send(slot(b)[0], *slot(b), l_b, (right, not_first))
            for _, slot in ROWG:
                for dev in (x_f, x_b):
                    send(slot(b)[0], *slot(b), dev, (right,))

    def x_forward(d):
        def one(q, conds):
            b = q * 4 + xb
            for _, slot in ROWG:
                arrived(*slot(b))
            for _, slot in ROWG:
                send(slot(b)[0], *slot(b), x_f, conds)

        if d == 0:
            one(p, ())
        else:
            left, right = p >= d, p + d <= 3
            pl.when(left)(lambda: one(p - d, (left,)))
            pl.when(right)(lambda: one(p + d, (right,)))

    def to_sibling(d):
        def one(q, conds):
            for b in (q * 4 + xf, q * 4 + mod(x + 2, 4)):
                for _, slot in ROWG:
                    arrived(*slot(b))
            part = h.at[pl.ds(q * 4, 4), core]
            send(part, part, hs_sem.at[q], lambda: h.at[pl.ds(0, 4), 0], sib, conds)
            part = o.at[pl.ds(q * 4, 4), core]
            send(part, part, os_sem.at[q], lambda: o.at[pl.ds(0, 4), 0], sib, conds)

        if d == 0:
            local[2].wait()
            local[3].wait()
            one(p, ())
        else:
            left, right = p >= d, p + d <= 3
            pl.when(left)(lambda: one(p - d, (left,)))
            pl.when(right)(lambda: one(p + d, (right,)))

    def zy(slot, b):
        arrived(*slot(b))
        for dev in (y_f, y_b):
            send(slot(b)[0], *slot(b), dev)

    def z_first(slot):
        b = zb * 4 + y
        arrived(*slot(b))
        send(slot(b)[0], *slot(b), z_f)
        for dev in (y_f, y_b):
            send(slot(b)[0], *slot(b), dev)
        zy(slot, zf * 4 + y)

    def z_second(slot):
        zy(slot, mod(zh + 2, 4) * 4 + y)

    def y_forward(slot, q):
        b = q * 4 + yb
        arrived(*slot(b))
        send(slot(b)[0], *slot(b), y_f)

    def y_last(slot, q):
        for b in (q * 4 + yf, q * 4 + mod(y + 2, 4)):
            arrived(*slot(b))

    z2 = mod(zh + 2, 4)
    line(1)
    z_first(aislot)
    x_forward(0)
    y_forward(aislot, zh)
    y_forward(ahslot, zh)
    line(2)
    x_forward(1)
    z_second(aislot)
    y_forward(aislot, zb)
    y_forward(aislot, zf)
    to_sibling(0)
    line(3)
    x_forward(2)
    z_first(ahslot)
    y_forward(aislot, z2)
    x_forward(3)
    to_sibling(1)
    y_forward(ahslot, zb)
    y_forward(ahslot, zf)
    to_sibling(2)
    to_sibling(3)

    local[0].wait()
    for q in (zh, zb, zf, z2):
        y_last(aislot, q)
    for q in range(4):
        part = h.at[pl.ds(q * 4, 4), 1 - core]
        arrived(part, hs_sem.at[q])
        part = o.at[pl.ds(q * 4, 4), 1 - core]
        arrived(part, os_sem.at[q])

    def product(a, b):
        return lax.dot_general(a, b, (((0,), (0,)), ((), ())), preferred_element_type=F32)

    lhs = ai[...].reshape(1024, 256)

    def up_tile(n, carry):
        cols = pl.ds(pl.multiple_of(n * 512, 512), 512)
        gu[:, cols] = product(lhs, h[:, :, :, cols].reshape(1024, 512))
        return carry

    z_second(ahslot)
    lax.fori_loop(0, 4, up_tile, 0)
    y_forward(ahslot, z2)

    def up_squares(j, sums):
        cols = pl.ds(pl.multiple_of(j * 128, 128), 128)
        g = gu[:, cols]
        sq = g * g + EPS_SQUARE
        cpart[pl.ds(j, 1), :] = jnp.sum(sq, axis=0, keepdims=True)
        return sums + sq

    sums = lax.fori_loop(0, 16, up_squares, jnp.zeros((256, 128), F32))
    for a in range(2):
        rpart[8 + a : 9 + a, :] = jnp.sum(
            jnp.transpose(sums[a * 128 : a * 128 + 128]), axis=0, keepdims=True
        )

    local[1].wait()

    def down_part(q, first):
        b = pl.ds(q * 4, 4)
        term = product(ah[b].reshape(256, 1024), o[b].reshape(256, 512))
        if first:
            gd[...] = term
        else:
            gd[...] += term

    for i, q in enumerate((zh, zb, zf, z2)):
        y_last(ahslot, q)
        down_part(q, i == 0)

    ctotal = jnp.zeros((8, 512), F32)
    for a in range(8):
        g = gd[a * 128 : a * 128 + 128, :]
        sq = g * g + EPS_SQUARE
        ctotal = ctotal + jnp.sum(sq.reshape(16, 8, 512), axis=0)
        lanes = sq[:, 0:128] + sq[:, 128:256] + sq[:, 256:384] + sq[:, 384:512]
        rpart[a : a + 1, :] = jnp.sum(jnp.transpose(lanes), axis=0, keepdims=True)
    csum = jnp.sum(ctotal, axis=0, keepdims=True)
    for j in range(4):
        cpart[16 + j : 17 + j, :] = csum[:, j * 128 : j * 128 + 128]

    def exchange(part, buf, ssem, rsem, n, me, where):
        def start(k, carry):
            to = mod(me + k, n)
            pltpu.make_async_remote_copy(
                part, buf.at[me], ssem.at[k], rsem.at[me], where(to), MESH
            ).start()
            return carry

        lax.fori_loop(1, n, start, 0)

    def finish(part, buf, ssem, rsem, n, me):
        def wait(k, carry):
            frm = mod(me + k, n)
            pltpu.make_async_remote_copy(
                buf.at[frm], buf.at[frm], ssem.at[k], rsem.at[frm], sib, MESH
            ).wait_recv()
            return carry

        lax.fori_loop(1, n, wait, 0)

    def finish_sends(part, buf, ssem, rsem, n, me):
        def wait(k, carry):
            pltpu.make_async_remote_copy(
                part, buf.at[me], ssem.at[k], rsem.at[me], sib, MESH
            ).wait_send()
            return carry

        lax.fori_loop(1, n, wait, 0)

    to_row = lambda k: (k, c)
    to_col = lambda k: (r, k)
    exchange(cpart, cbuf, c_send, c_recv, ROWS, r, to_row)
    exchange(rpart, rbuf, r_send, r_recv, COLS, c, to_col)
    cbuf[r] = cpart[...]
    rbuf[c] = rpart[...]

    for like, k, conds in sends:
        when(conds, lambda: pltpu.make_async_remote_copy(
            like(), like(), send_sem.at[k], loc_sem.at[0], sib, MESH).wait_send())
    for copy in local[4:]:
        copy.wait()

    finish(rpart, rbuf, r_send, r_recv, COLS, c)
    row_sum = jnp.sum(rbuf[...], axis=0)
    keep, take = DECAY, 1.0 - DECAY
    rn_d = keep * rstate[0:8, :] + take * (row_sum[0:8] / D)
    rn_u = keep * rstate[8:10, :] + take * (row_sum[8:10] / FF)
    rnew[0:8, :] = rn_d
    rnew[8:10, :] = rn_u
    rroot_d = lax.rsqrt(rn_d)
    rroot_u = lax.rsqrt(rn_u)
    for a in range(8):
        rbd[a * 128 : a * 128 + 128, :] = jnp.transpose(
            jnp.broadcast_to(rroot_d[a : a + 1, :], (128, 128))
        )
    for a in range(2):
        rbu[a * 128 : a * 128 + 128, :] = jnp.transpose(
            jnp.broadcast_to(rroot_u[a : a + 1, :], (128, 128))
        )

    finish(cpart, cbuf, c_send, c_recv, ROWS, r)
    col_sum = jnp.sum(cbuf[...], axis=0)
    cn_u = keep * cstate[0:16, :] + take * (col_sum[0:16] / D)
    cn_d = keep * cstate[16:20, :] + take * (col_sum[16:20] / FF)
    cnew[0:16, :] = cn_u
    cnew[16:20, :] = cn_d
    cstate[0:16, :] = lax.rsqrt(cn_u)
    cstate[16:20, :] = lax.rsqrt(cn_d)

    outs = [
        pltpu.make_async_copy(rnew.at[pl.ds(8, 2)], rnu_out, out_sem.at[0]),
        pltpu.make_async_copy(rnew.at[pl.ds(0, 8)], rnd_out, out_sem.at[1]),
        pltpu.make_async_copy(cnew.at[pl.ds(0, 16)], cnu_out, out_sem.at[2]),
        pltpu.make_async_copy(cnew.at[pl.ds(16, 4)], cnd_out, out_sem.at[3]),
        pltpu.make_async_copy(uu, uu_out, out_sem.at[4]),
        pltpu.make_async_copy(ud, ud_out, out_sem.at[5]),
    ]
    for copy in outs[:4]:
        copy.start()

    def up_raw(j, total):
        cols = pl.ds(pl.multiple_of(j * 128, 128), 128)
        raw = gu[:, cols] * rbu[...] * cstate[pl.ds(j, 1), :]
        return total + jnp.sum((raw * raw).reshape(32, 8, 128), axis=0)

    tu = lax.fori_loop(0, 16, up_raw, jnp.zeros((8, 128), F32))

    def down_raw(a, total):
        rows = pl.ds(pl.multiple_of(a * 128, 128), 128)
        for j in range(4):
            cols = slice(j * 128, j * 128 + 128)
            raw = gd[rows, cols] * rbd[rows, :] * cstate[16 + j : 17 + j, :]
            total = total + jnp.sum((raw * raw).reshape(16, 8, 128), axis=0)
        return total

    td = lax.fori_loop(0, 8, down_raw, jnp.zeros((8, 128), F32))
    tpart[0] = tu
    tpart[1] = td

    exchange(tpart, tbuf1, t1_send, t1_recv, COLS, c, to_col)
    tbuf1[c] = tpart[...]
    finish_sends(rpart, rbuf, r_send, r_recv, COLS, c)
    finish_sends(cpart, cbuf, c_send, c_recv, ROWS, r)
    finish(tpart, tbuf1, t1_send, t1_recv, COLS, c)
    tpart2[...] = jnp.sum(tbuf1[...], axis=0)
    exchange(tpart2, tbuf2, t2_send, t2_recv, ROWS, r, to_row)
    tbuf2[r] = tpart2[...]
    finish_sends(tpart, tbuf1, t1_send, t1_recv, COLS, c)
    finish(tpart2, tbuf2, t2_send, t2_recv, ROWS, r)
    totals = jnp.sum(tbuf2[...], axis=0)
    size = float(D) * float(FF)

    def scale_of(t):
        total = jnp.sum(jnp.sum(t, axis=0, keepdims=True), axis=1, keepdims=True)
        return 1.0 / jnp.maximum(CLIP_FLOOR, jnp.sqrt(total / size))

    scale_u = scale_of(totals[0])
    scale_d = scale_of(totals[1])
    cstate[0:16, :] = cstate[0:16, :] * scale_u
    cstate[16:20, :] = cstate[16:20, :] * scale_d

    def up_write(j, carry):
        cols = pl.ds(pl.multiple_of(j * 128, 128), 128)
        uu[:, cols] = (gu[:, cols] * rbu[...] * cstate[pl.ds(j, 1), :]).astype(BF16)
        return carry

    lax.fori_loop(0, 16, up_write, 0)
    outs[4].start()

    def down_write(a, carry):
        rows = pl.ds(pl.multiple_of(a * 128, 128), 128)
        for j in range(4):
            cols = slice(j * 128, j * 128 + 128)
            ud[rows, cols] = (
                gd[rows, cols] * rbd[rows, :] * cstate[16 + j : 17 + j, :]
            ).astype(BF16)
        return carry

    lax.fori_loop(0, 8, down_write, 0)
    outs[5].start()
    finish_sends(tpart2, tbuf2, t2_send, t2_recv, ROWS, r)
    for copy in outs:
        copy.wait()


def on_device(ai, h, ah, o, rsu, csu, rsd, csd):
    dma = pltpu.SemaphoreType.DMA
    any_ = pl.BlockSpec(memory_space=pl.ANY)

    res = pl.pallas_call(
        kernel,
        out_shape=(
            jax.ShapeDtypeStruct((256, 2048), BF16),
            jax.ShapeDtypeStruct((2, 128), F32),
            jax.ShapeDtypeStruct((16, 128), F32),
            jax.ShapeDtypeStruct((1024, 512), BF16),
            jax.ShapeDtypeStruct((8, 128), F32),
            jax.ShapeDtypeStruct((4, 128), F32),
        ),
        in_specs=[any_] * 8,
        out_specs=[any_] * 6,
        scratch_shapes=[
            pltpu.VMEM((NB, 64, 256), BF16),
            pltpu.VMEM((NB, 64, 1024), BF16),
            pltpu.VMEM((NB, 2, 32, 2048), BF16),
            pltpu.VMEM((NB, 2, 32, 512), BF16),
            pltpu.VMEM((256, 2048), F32),
            pltpu.VMEM((1024, 512), F32),
            pltpu.VMEM((256, 2048), BF16),
            pltpu.VMEM((1024, 512), BF16),
            pltpu.VMEM((256, 128), F32),
            pltpu.VMEM((1024, 128), F32),
            pltpu.VMEM((16, 128), F32),
            pltpu.VMEM((24, 128), F32),
            pltpu.VMEM((16, 128), F32),
            pltpu.VMEM((24, 128), F32),
            pltpu.VMEM((16, 128), F32),
            pltpu.VMEM((24, 128), F32),
            pltpu.VMEM((COLS, 16, 128), F32),
            pltpu.VMEM((ROWS, 24, 128), F32),
            pltpu.VMEM((2, 8, 128), F32),
            pltpu.VMEM((COLS, 2, 8, 128), F32),
            pltpu.VMEM((2, 8, 128), F32),
            pltpu.VMEM((ROWS, 2, 8, 128), F32),
            dma((NB,)), dma((NB,)), dma((NB,)), dma((NB,)), dma((4,)), dma((4,)),
            dma((NSEND,)), dma((8,)), dma((6,)),
            dma((COLS,)), dma((ROWS,)), dma((COLS,)), dma((ROWS,)),
            dma((COLS,)), dma((COLS,)), dma((ROWS,)), dma((ROWS,)),
        ],
        compiler_params=pltpu.CompilerParams(
            collective_id=0, has_side_effects=True, vmem_limit_bytes=40 * 1024 * 1024
        ),
        cost_estimate=pl.CostEstimate(
            flops=2 * 2 * 1024 * 256 * 2048, bytes_accessed=3 << 20, transcendentals=0
        ),
    )(ai, h, ah, o, rsu.reshape(2, 128), csu.reshape(16, 128), rsd.reshape(8, 128), csd.reshape(4, 128))
    uu, rnu, cnu, ud, rnd, cnd = res
    return (uu, rnu.reshape(256), cnu.reshape(2048), ud, rnd.reshape(1024), cnd.reshape(512))


def solution(mesh):
    in_specs = (
        P("col", "row"),
        P("row", "col"),
        P("col", "row"),
        P("row", "col"),
        P("row"),
        P("col"),
        P("row"),
        P("col"),
    )
    out_specs = (P("row", "col"), P("row"), P("col"), P("row", "col"), P("row"), P("col"))
    return jax.shard_map(
        on_device, mesh=mesh, in_specs=in_specs, out_specs=out_specs, check_vma=False
    )
```

```python
import jax
import jax.numpy as jnp
from jax import lax
from jax.experimental import pallas as pl
from jax.experimental.pallas import tpu as pltpu
from jax.sharding import PartitionSpec as P

D = 8192
FF = 32768
DECAY = 1.0 - 10.0 ** (-0.8)
EPS_SQUARE = 1e-30
CLIP_FLOOR = 0.1

NB = 16
ROWS = 32
COLS = 16
AHC = 2
F32 = jnp.float32
BF16 = jnp.bfloat16
MESH = pl.DeviceIdType.MESH
NSEND = 200
VMEM_MB = 57


def mod(a, n):
    return lax.rem(a + n, n)


def kernel(
    ai_in, h_in, ah_in, o_in, rsu_in, csu_in, rsd_in, csd_in,
    uu, rnu, cnu, ud, rnd, cnd,
    ai, ah, h, o, gu, gd, rbu, rbd, rsu, csu, rsd, csd, cru, crd,
    rpu, cpu, cpu2, rpd, cpd, rbufu, cbufu, cbufu2, rbufd, cbufd, tp1, tbuf1, tp2, tbuf2,
    ai_sem, ah_sem, h_sem, o_sem, hs_sem, os_sem, send_sem, loc_sem,
    rd_sem, cd_sem, ru_sem, cu1_sem, cu2_sem, t1_sem, t2_sem,
):
    r = lax.axis_index("row")
    c = lax.axis_index("col")
    core = lax.rem(r, 2)
    x = lax.rem(r // 2, 4)
    p = r // 8
    y = lax.rem(c, 4)
    zh = c // 4
    s = 1 - 2 * core

    def row_at(zl_, x_, core_):
        return (zl_ * 8 + x_ * 2 + core_, c)

    def col_at(zh_, y_):
        return (r, zh_ * 4 + y_)

    zf, zb, z2 = mod(zh + s, 4), mod(zh - s, 4), mod(zh + 2, 4)
    xs = [row_at(p, mod(x + i, 4), core) for i in (2, 1, 3)]
    ys = [col_at(zh, mod(y + i, 4)) for i in (2, 1, 3)]
    z_f, z_b = col_at(zf, y), col_at(zb, y)
    l_f, l_b = row_at(mod(p + 1, 4), x, core), row_at(mod(p - 1, 4), x, core)
    sib = row_at(p, x, 1 - core)

    barrier = pltpu.get_barrier_semaphore()
    for dev in (z_f, z_b, l_f, l_b, *xs, *ys, sib):
        pl.semaphore_signal(barrier, inc=1, device_id=dev, device_id_type=MESH)
    pl.semaphore_wait(barrier, 11)

    sends = []

    def send(src, dst, recv, like, dev, conds=()):
        k = len(sends)
        pltpu.make_async_remote_copy(src, dst, send_sem.at[k], recv, dev, MESH).start()
        sends.append((like, conds))

    def when(conds, f):
        if not conds:
            f()
        else:
            pl.when(conds[0])(lambda: when(conds[1:], f))

    def arrived(dst, recv, like=None):
        pltpu.make_async_remote_copy(dst, dst, send_sem.at[0], recv, sib, MESH).wait_recv()

    def hslot(b):
        return h.at[b, core], h_sem.at[b], lambda: h.at[0, 0]

    def oslot(b):
        return o.at[b, core], o_sem.at[b], lambda: o.at[0, 0]

    def aislot(b):
        return ai.at[b], ai_sem.at[b], lambda: ai.at[0]

    AHT = 64 // AHC

    def ahslot(t):
        part = pl.ds(t * AHT, AHT)

        def slot(b):
            return ah.at[b, part], ah_sem.at[b, t], lambda: ah.at[0, part]

        return slot

    not_last, not_first = p < 3, p > 0
    own_r, own_c = p * 4 + x, c
    ah_own = [ah_in.at[pl.ds(t * AHT, AHT)] for t in range(AHC)]

    def line_own(src, slot):
        @pl.when(not_last)
        def _():
            send(src, *slot(own_r), l_f, (not_last,))

        @pl.when(not_first)
        def _():
            send(src, *slot(own_r), l_b, (not_first,))

    def spread(src, slot, b, devs, conds=()):
        for dev in devs:
            send(src, *slot(b), dev, conds)

    line_own(h_in, hslot)
    spread(ah_own[0], ahslot(0), own_c, (z_f, z_b))
    line_own(o_in, oslot)
    spread(h_in, hslot, own_r, xs)
    for t in range(AHC):
        spread(ah_own[t], ahslot(t), own_c, ys)
    spread(o_in, oslot, own_r, xs)
    spread(ai_in, aislot, own_c, ys)

    local = [
        pltpu.make_async_copy(ai_in, ai.at[own_c], loc_sem.at[0]),
        pltpu.make_async_copy(ah_in, ah.at[own_c], loc_sem.at[1]),
        pltpu.make_async_copy(h_in, h.at[own_r, core], loc_sem.at[2]),
        pltpu.make_async_copy(o_in, o.at[own_r, core], loc_sem.at[3]),
        pltpu.make_async_copy(rsu_in, rsu, loc_sem.at[4]),
        pltpu.make_async_copy(rsd_in, rsd, loc_sem.at[5]),
        pltpu.make_async_copy(csu_in, csu, loc_sem.at[6]),
        pltpu.make_async_copy(csd_in, csd, loc_sem.at[7]),
    ]
    for copy in local:
        copy.start()

    def line(slot, d):
        left, right = p >= d, p + d <= 3

        def one(b, further, dev, conds):
            arrived(*slot(b))
            if d < 3:
                @pl.when(further)
                def _():
                    send(slot(b)[0], *slot(b), dev, conds + (further,))
            spread(slot(b)[0], slot, b, xs, conds)

        pl.when(left)(lambda: one((p - d) * 4 + x, not_last, l_f, (left,)))
        pl.when(right)(lambda: one((p + d) * 4 + x, not_first, l_b, (right,)))

    def z_one(slot, zz, onward=False):
        b = zz * 4 + y
        arrived(*slot(b))
        if onward:
            send(slot(b)[0], *slot(b), z_f)
        spread(slot(b)[0], slot, b, ys)

    def z_first(slot):
        z_one(slot, zb, True)
        z_one(slot, zf)

    def z_second(slot):
        z_one(slot, z2)

    def to_sibling(d):
        def one(q, conds):
            for i in (1, 3, 2):
                b = q * 4 + mod(x + i, 4)
                arrived(*hslot(b))
                arrived(*oslot(b))
            for buf, sem in ((h, hs_sem), (o, os_sem)):
                part = buf.at[pl.ds(q * 4, 4), core]
                send(part, part, sem.at[q], lambda buf=buf: buf.at[pl.ds(0, 4), 0], sib, conds)

        if d == 0:
            local[2].wait()
            local[3].wait()
            one(p, ())
        else:
            left, right = p >= d, p + d <= 3
            pl.when(left)(lambda: one(p - d, (left,)))
            pl.when(right)(lambda: one(p + d, (right,)))

    def y_last(slot, q):
        for i in (1, 3, 2):
            arrived(*slot(q * 4 + mod(y + i, 4)))

    line(hslot, 1)
    z_first(ahslot(0))
    spread(ah_own[1], ahslot(1), own_c, (z_f, z_b))
    line(oslot, 1)
    line(hslot, 2)
    z_first(ahslot(1))
    spread(ai_in, aislot, own_c, (z_f, z_b))
    line(oslot, 2)
    z_second(ahslot(0))
    line(hslot, 3)
    to_sibling(0)
    line(oslot, 3)
    z_first(aislot)
    z_second(ahslot(1))
    to_sibling(1)
    z_second(aislot)
    to_sibling(2)
    to_sibling(3)
    def product(a, b):
        return lax.dot_general(a, b, (((0,), (0,)), ((), ())), preferred_element_type=F32)

    def start(part, buf, sem, n, me, where):
        def one(k, carry):
            pltpu.make_async_remote_copy(
                part, buf.at[me], sem.at[1, k], sem.at[0, me], where(mod(me + k, n)), MESH
            ).start()
            return carry

        lax.fori_loop(1, n, one, 0)
        buf[me] = part[...]

    def finish(buf, sem, n, me):
        def one(k, carry):
            frm = mod(me + k, n)
            pltpu.make_async_remote_copy(
                buf.at[frm], buf.at[frm], sem.at[1, k], sem.at[0, frm], sib, MESH
            ).wait_recv()
            return carry

        lax.fori_loop(1, n, one, 0)
        return jnp.sum(buf[...], axis=0)

    def finish_sends(part, sem, n):
        def one(k, carry):
            pltpu.make_async_remote_copy(
                part, part, sem.at[1, k], sem.at[0, 0], sib, MESH
            ).wait_send()
            return carry

        lax.fori_loop(1, n, one, 0)

    to_row = lambda k: (k, c)
    to_col = lambda k: (r, k)
    in_x = lambda k: (p * 8 + k, c)
    in_line = lambda k: (k * 8 + lax.rem(r, 8), c)
    in_plane = lambda k: (p * 8 + lax.rem(k, 8), zh * 4 + k // 8)
    in_z = lambda k: (lax.rem(k, 4) * 8 + lax.rem(r, 8), (k // 4) * 4 + y)


    local[1].wait()
    for q in range(4):
        arrived(o.at[pl.ds(q * 4, 4), 1 - core], os_sem.at[q])
    for q in (zh, zb, zf, z2):
        for t in range(AHC):
            y_last(ahslot(t), q)
    lhs_down = ah[...].reshape(1024, 1024)
    gd[...] = product(lhs_down, o[...].reshape(1024, 512))

    ctotal = jnp.zeros((8, 512), F32)
    for a in range(8):
        g = gd[a * 128 : a * 128 + 128, :]
        sq = g * g + EPS_SQUARE
        ctotal = ctotal + jnp.sum(sq.reshape(16, 8, 512), axis=0)
        lanes = sq[:, 0:128] + sq[:, 128:256] + sq[:, 256:384] + sq[:, 384:512]
        rpd[a : a + 1, :] = jnp.sum(jnp.transpose(lanes), axis=0, keepdims=True)
    csum = jnp.sum(ctotal, axis=0, keepdims=True)
    for j in range(4):
        cpd[j : j + 1, :] = csum[:, j * 128 : j * 128 + 128]

    start(rpd, rbufd, rd_sem, COLS, c, to_col)
    start(cpd, cbufd, cd_sem, ROWS, r, to_row)

    local[0].wait()
    for q in range(4):
        arrived(h.at[pl.ds(q * 4, 4), 1 - core], hs_sem.at[q])
    for q in (zh, zb, zf, z2):
        y_last(aislot, q)
    lhs = ai[...].reshape(1024, 256)

    def up_tile(n, carry):
        cols = pl.ds(pl.multiple_of(n * 512, 512), 512)
        gu[:, cols] = product(lhs, h[:, :, :, cols].reshape(1024, 512))
        return carry

    lax.fori_loop(0, 4, up_tile, 0)

    def up_squares(j, sums):
        cols = pl.ds(pl.multiple_of(j * 128, 128), 128)
        g = gu[:, cols]
        sq = g * g + EPS_SQUARE
        cpu[pl.ds(j, 1), :] = jnp.sum(sq, axis=0, keepdims=True)
        return sums + sq

    sums = lax.fori_loop(0, 16, up_squares, jnp.zeros((256, 128), F32))
    for a in range(2):
        rpu[a : a + 1, :] = jnp.sum(
            jnp.transpose(sums[a * 128 : a * 128 + 128]), axis=0, keepdims=True
        )


    start(cpu, cbufu, cu1_sem, 8, x * 2 + core, in_x)
    start(rpu, rbufu, ru_sem, COLS, c, to_col)

    cpu2[...] = finish(cbufu, cu1_sem, 8, x * 2 + core)
    start(cpu2, cbufu2, cu2_sem, 4, p, in_line)

    for k, (like, conds) in enumerate(sends):
        when(conds, lambda: pltpu.make_async_remote_copy(
            like(), like(), send_sem.at[k], loc_sem.at[0], sib, MESH).wait_send())
    for copy in local[4:]:
        copy.wait()

    keep, take = DECAY, 1.0 - DECAY
    cn = keep * csd[...] + take * (finish(cbufd, cd_sem, ROWS, r) / FF)
    cnd[...] = cn
    crd[...] = lax.rsqrt(cn)
    rn = keep * rsd[...] + take * (finish(rbufd, rd_sem, COLS, c) / D)
    rnd[...] = rn
    rroot = lax.rsqrt(rn)
    for a in range(8):
        rbd[a * 128 : a * 128 + 128, :] = jnp.transpose(
            jnp.broadcast_to(rroot[a : a + 1, :], (128, 128))
        )

    def down_raw(a, total):
        rows = pl.ds(pl.multiple_of(a * 128, 128), 128)
        for j in range(4):
            raw = gd[rows, j * 128 : j * 128 + 128] * rbd[rows, :] * crd[j : j + 1, :]
            total = total + jnp.sum((raw * raw).reshape(16, 8, 128), axis=0)
        return total

    td = lax.fori_loop(0, 8, down_raw, jnp.zeros((8, 128), F32))
    tp1[1:2, :] = jnp.sum(td, axis=0, keepdims=True)

    rn = keep * rsu[...] + take * (finish(rbufu, ru_sem, COLS, c) / FF)
    rnu[...] = rn
    rroot = lax.rsqrt(rn)
    for a in range(2):
        rbu[a * 128 : a * 128 + 128, :] = jnp.transpose(
            jnp.broadcast_to(rroot[a : a + 1, :], (128, 128))
        )
    cn = keep * csu[...] + take * (finish(cbufu2, cu2_sem, 4, p) / D)
    cnu[...] = cn
    cru[...] = lax.rsqrt(cn)

    def up_raw(j, total):
        cols = pl.ds(pl.multiple_of(j * 128, 128), 128)
        raw = gu[:, cols] * rbu[...] * cru[pl.ds(j, 1), :]
        return total + jnp.sum((raw * raw).reshape(32, 8, 128), axis=0)

    tu = lax.fori_loop(0, 16, up_raw, jnp.zeros((8, 128), F32))
    tp1[0:1, :] = jnp.sum(tu, axis=0, keepdims=True)

    place = y * 8 + x * 2 + core
    start(tp1, tbuf1, t1_sem, 32, place, in_plane)
    finish_sends(cpu, cu1_sem, 8)
    finish_sends(rpu, ru_sem, COLS)
    finish_sends(cpu2, cu2_sem, 4)
    finish_sends(rpd, rd_sem, COLS)
    finish_sends(cpd, cd_sem, ROWS)
    tp2[...] = finish(tbuf1, t1_sem, 32, place)
    start(tp2, tbuf2, t2_sem, 16, zh * 4 + p, in_z)
    finish_sends(tp1, t1_sem, 32)
    totals = finish(tbuf2, t2_sem, 16, zh * 4 + p)
    rms = jnp.sqrt(jnp.sum(totals, axis=1, keepdims=True) / (float(D) * float(FF)))
    scale = 1.0 / jnp.maximum(CLIP_FLOOR, rms)
    cru[...] = cru[...] * scale[0:1, :]
    crd[...] = crd[...] * scale[1:2, :]

    def up_write(j, carry):
        cols = pl.ds(pl.multiple_of(j * 128, 128), 128)
        uu[:, cols] = (gu[:, cols] * rbu[...] * cru[pl.ds(j, 1), :]).astype(BF16)
        return carry

    lax.fori_loop(0, 16, up_write, 0)

    def down_write(a, carry):
        rows = pl.ds(pl.multiple_of(a * 128, 128), 128)
        for j in range(4):
            cols = slice(j * 128, j * 128 + 128)
            ud[rows, cols] = (gd[rows, cols] * rbd[rows, :] * crd[j : j + 1, :]).astype(BF16)
        return carry

    lax.fori_loop(0, 8, down_write, 0)
    finish_sends(tp2, t2_sem, 16)


def write_out(*refs):
    ins, outs, sem = refs[:6], refs[6:12], refs[12]
    copies = [
        pltpu.make_async_copy(a, b, sem.at[i]) for i, (a, b) in enumerate(zip(ins, outs))
    ]
    for copy in copies:
        copy.start()
    for copy in copies:
        copy.wait()


SHAPES = (
    ((256, 2048), BF16),
    ((2, 128), F32),
    ((16, 128), F32),
    ((1024, 512), BF16),
    ((8, 128), F32),
    ((4, 128), F32),
)


def on_device(ai, h, ah, o, rsu, csu, rsd, csd):
    dma = pltpu.SemaphoreType.DMA
    any_ = pl.BlockSpec(memory_space=pl.ANY)
    vmem = pl.BlockSpec(memory_space=pltpu.VMEM)
    f32 = lambda *shape: pltpu.VMEM(shape, F32)
    bf16 = lambda *shape: pltpu.VMEM(shape, BF16)
    res = pl.pallas_call(
        kernel,
        out_shape=tuple(pltpu.VMEM(shape, dtype) for shape, dtype in SHAPES),
        in_specs=[any_] * 8,
        out_specs=[vmem] * 6,
        scratch_shapes=[
            bf16(NB, 64, 256), bf16(NB, 64, 1024), bf16(NB, 2, 32, 2048), bf16(NB, 2, 32, 512),
            f32(256, 2048), f32(1024, 512), f32(256, 128), f32(1024, 128),
            f32(2, 128), f32(16, 128), f32(8, 128), f32(4, 128), f32(16, 128), f32(4, 128),
            f32(2, 128), f32(16, 128), f32(16, 128), f32(8, 128), f32(4, 128),
            f32(COLS, 2, 128), f32(8, 16, 128), f32(4, 16, 128), f32(COLS, 8, 128), f32(ROWS, 4, 128),
            f32(2, 128), f32(32, 2, 128), f32(2, 128), f32(16, 2, 128),
            dma((NB,)), dma((NB, AHC)), dma((NB,)), dma((NB,)), dma((4,)), dma((4,)),
            dma((NSEND,)), dma((8,)),
            dma((2, COLS)), dma((2, ROWS)), dma((2, COLS)), dma((2, 8)), dma((2, 4)),
            dma((2, 32)), dma((2, 16)),
        ],
        compiler_params=pltpu.CompilerParams(
            collective_id=0, has_side_effects=True, vmem_limit_bytes=VMEM_MB * 1024 * 1024
        ),
        cost_estimate=pl.CostEstimate(
            flops=2 * 2 * 1024 * 256 * 2048, bytes_accessed=3 << 20, transcendentals=0
        ),
    )(ai, h, ah, o, rsu.reshape(2, 128), csu.reshape(16, 128), rsd.reshape(8, 128), csd.reshape(4, 128))
    uu, rnu, cnu, ud, rnd, cnd = pl.pallas_call(
        write_out,
        out_shape=tuple(pltpu.HBM(shape, dtype) for shape, dtype in SHAPES),
        in_specs=[vmem] * 6,
        out_specs=[pl.BlockSpec(memory_space=pltpu.HBM)] * 6,
        scratch_shapes=[dma((6,))],
        compiler_params=pltpu.CompilerParams(has_side_effects=True),
    )(*[pltpu.with_memory_space_constraint(t, pltpu.VMEM) for t in res])
    return (uu, rnu.reshape(256), cnu.reshape(2048), ud, rnd.reshape(1024), cnd.reshape(512))


def solution(mesh):
    in_specs = (
        P("col", "row"),
        P("row", "col"),
        P("col", "row"),
        P("row", "col"),
        P("row"),
        P("col"),
        P("row"),
        P("col"),
    )
    out_specs = (P("row", "col"), P("row"), P("col"), P("row", "col"), P("row"), P("col"))
    return jax.shard_map(
        on_device, mesh=mesh, in_specs=in_specs, out_specs=out_specs, check_vma=False
    )
```

```python
import jax
import jax.numpy as jnp
from jax import lax
from jax.experimental import pallas as pl
from jax.experimental.pallas import tpu as pltpu
from jax.sharding import PartitionSpec as P

D = 8192
FF = 32768
DECAY = 1.0 - 10.0 ** (-0.8)
EPS_SQUARE = 1e-30
CLIP_FLOOR = 0.1

NB = 16
ROWS = 32
COLS = 16
HC = 1
AHC = 2
F32 = jnp.float32
BF16 = jnp.bfloat16
MESH = pl.DeviceIdType.MESH
NSEND = 240
VMEM_MB = 57


def mod(a, n):
    return lax.rem(a + n, n)


def kernel(
    ai_in, h_in, ah_in, o_in, rsu_in, csu_in, rsd_in, csd_in,
    uu, rnu, cnu, ud, rnd, cnd,
    ai, ah, h, o, gu, gd, rbu, rbd, rsu, csu, rsd, csd, cru, crd,
    rpu, cpu, cpu2, rpd, cpd, cpd2, rbufu, cbufu, cbufu2, rbufd, cbufd, cbufd2, tp1, tbuf1, tp2, tbuf2,
    ai_sem, ah_sem, h_sem, o_sem, hs_sem, os_sem, send_sem, loc_sem,
    rd_sem, cd1_sem, cd2_sem, ru_sem, cu1_sem, cu2_sem, t1_sem, t2_sem,
):
    r = lax.axis_index("row")
    c = lax.axis_index("col")
    core = lax.rem(r, 2)
    x = lax.rem(r // 2, 4)
    p = r // 8
    y = lax.rem(c, 4)
    zh = c // 4
    s = 1 - 2 * core

    def row_at(zl_, x_, core_):
        return (zl_ * 8 + x_ * 2 + core_, c)

    def col_at(zh_, y_):
        return (r, zh_ * 4 + y_)

    zf, zb, z2 = mod(zh + s, 4), mod(zh - s, 4), mod(zh + 2, 4)
    xs = [row_at(p, mod(x + i, 4), core) for i in (2, 1, 3)]
    ys = [col_at(zh, mod(y + i, 4)) for i in (2, 1, 3)]
    z_f, z_b = col_at(zf, y), col_at(zb, y)
    l_f, l_b = row_at(mod(p + 1, 4), x, core), row_at(mod(p - 1, 4), x, core)
    sib = row_at(p, x, 1 - core)

    barrier = pltpu.get_barrier_semaphore()
    for dev in (z_f, z_b, l_f, l_b, *xs, *ys, sib):
        pl.semaphore_signal(barrier, inc=1, device_id=dev, device_id_type=MESH)
    pl.semaphore_wait(barrier, 11)

    sends = []

    def send(src, dst, recv, like, dev, conds=()):
        k = len(sends)
        pltpu.make_async_remote_copy(src, dst, send_sem.at[k], recv, dev, MESH).start()
        sends.append((like, conds))

    def when(conds, f):
        if not conds:
            f()
        else:
            pl.when(conds[0])(lambda: when(conds[1:], f))

    def arrived(dst, recv, like=None):
        pltpu.make_async_remote_copy(dst, dst, send_sem.at[0], recv, sib, MESH).wait_recv()

    HT = 32 // HC

    def hslot(t):
        part = pl.ds(t * HT, HT)

        def slot(b):
            return h.at[b, core, part], h_sem.at[b, t], lambda: h.at[0, 0, part]

        return slot

    def oslot(b):
        return o.at[b, core], o_sem.at[b], lambda: o.at[0, 0]

    def aislot(b):
        return ai.at[b], ai_sem.at[b], lambda: ai.at[0]

    AHT = 64 // AHC

    def ahslot(t):
        part = pl.ds(t * AHT, AHT)

        def slot(b):
            return ah.at[b, part], ah_sem.at[b, t], lambda: ah.at[0, part]

        return slot

    not_last, not_first = p < 3, p > 0
    own_r, own_c = p * 4 + x, c
    h_own = [h_in.at[pl.ds(t * HT, HT)] for t in range(HC)]
    ah_own = [ah_in.at[pl.ds(t * AHT, AHT)] for t in range(AHC)]

    def line_own(src, slot):
        @pl.when(not_last)
        def _():
            send(src, *slot(own_r), l_f, (not_last,))

        @pl.when(not_first)
        def _():
            send(src, *slot(own_r), l_b, (not_first,))

    def spread(src, slot, b, devs, conds=()):
        for dev in devs:
            send(src, *slot(b), dev, conds)

    line_own(h_own[0], hslot(0))
    spread(ah_own[0], ahslot(0), own_c, (z_f, z_b))
    line_own(o_in, oslot)
    for t in range(HC):
        spread(h_own[t], hslot(t), own_r, xs)
    for t in range(AHC):
        spread(ah_own[t], ahslot(t), own_c, ys)
    spread(o_in, oslot, own_r, xs)
    spread(ai_in, aislot, own_c, ys)

    local = [
        pltpu.make_async_copy(ai_in, ai.at[own_c], loc_sem.at[0]),
        pltpu.make_async_copy(ah_in, ah.at[own_c], loc_sem.at[1]),
        pltpu.make_async_copy(h_in, h.at[own_r, core], loc_sem.at[2]),
        pltpu.make_async_copy(o_in, o.at[own_r, core], loc_sem.at[3]),
        pltpu.make_async_copy(rsu_in, rsu, loc_sem.at[4]),
        pltpu.make_async_copy(rsd_in, rsd, loc_sem.at[5]),
        pltpu.make_async_copy(csu_in, csu, loc_sem.at[6]),
        pltpu.make_async_copy(csd_in, csd, loc_sem.at[7]),
    ]
    for copy in local:
        copy.start()

    def line(slot, d):
        left, right = p >= d, p + d <= 3

        def one(b, further, dev, conds):
            arrived(*slot(b))
            if d < 3:
                @pl.when(further)
                def _():
                    send(slot(b)[0], *slot(b), dev, conds + (further,))
            spread(slot(b)[0], slot, b, xs, conds)

        pl.when(left)(lambda: one((p - d) * 4 + x, not_last, l_f, (left,)))
        pl.when(right)(lambda: one((p + d) * 4 + x, not_first, l_b, (right,)))

    def z_one(slot, zz, onward=False):
        b = zz * 4 + y
        arrived(*slot(b))
        if onward:
            send(slot(b)[0], *slot(b), z_f)
        spread(slot(b)[0], slot, b, ys)

    def z_first(slot):
        z_one(slot, zb, True)
        z_one(slot, zf)

    def z_second(slot):
        z_one(slot, z2)

    def to_sibling(buf, sem, slots, mine, d):
        def one(q, conds):
            for i in (1, 3, 2):
                for slot in slots:
                    arrived(*slot(q * 4 + mod(x + i, 4)))
            part = buf.at[pl.ds(q * 4, 4), core]
            send(part, part, sem.at[q], lambda: buf.at[pl.ds(0, 4), 0], sib, conds)

        if d == 0:
            mine.wait()
            one(p, ())
        else:
            left, right = p >= d, p + d <= 3
            pl.when(left)(lambda: one(p - d, (left,)))
            pl.when(right)(lambda: one(p + d, (right,)))

    def y_last(slot, q):
        for i in (1, 3, 2):
            arrived(*slot(q * 4 + mod(y + i, 4)))

    def product(a, b):
        return lax.dot_general(a, b, (((0,), (0,)), ((), ())), preferred_element_type=F32)


    def start(part, buf, sem, me, *groups):
        for first, last, where in groups:

            def one(k, carry, where=where):
                pltpu.make_async_remote_copy(
                    part, buf.at[me], sem.at[1], sem.at[0], where(k), MESH
                ).start()
                return carry

            lax.fori_loop(first, last, one, 0)
        buf[me] = part[...]

    def finish(buf, sem, n):
        others = buf.at[pl.ds(0, n - 1)]
        pltpu.make_async_remote_copy(others, others, sem.at[1], sem.at[0], sib, MESH).wait_recv()
        return jnp.sum(buf[...], axis=0)

    def finish_sends(buf, sem, n):
        others = buf.at[pl.ds(0, n - 1)]
        pltpu.make_async_remote_copy(others, others, sem.at[1], sem.at[0], sib, MESH).wait_send()

    on_x = x * 2 + core
    in_x = ((1, 8, lambda k: (p * 8 + lax.rem(on_x + k, 8), c)),)
    in_line = tuple((d, d + 1, lambda k: (lax.rem(p + k, 4) * 8 + on_x, c)) for d in (2, 1, 3))

    def around(d, first, last, group, base):
        at = group(d)
        return (first, last, lambda k: base(at, k))

    def col_of(d):
        return around(d, 1 if d == 0 else 0, 4, lambda d: mod(zh + d, 4) * 4, lambda at, k: (r, at + lax.rem(y + k, 4)))

    def plane_of(d):
        return around(d, 1 if d == 0 else 0, 8, lambda d: zh * 4 + mod(y + d, 4), lambda at, k: (p * 8 + lax.rem(on_x + k, 8), at))

    def z_of(d):
        return around(d, 1 if d == 0 else 0, 4, lambda d: mod(zh + d, 4) * 4 + y, lambda at, k: (lax.rem(p + k, 4) * 8 + on_x, at))

    in_col = [col_of(d) for d in (2, 1, 3, 0)]
    in_plane = [plane_of(d) for d in (2, 1, 3, 0)]
    in_z = [z_of(d) for d in (2, 1, 3, 0)]

    def down_part(i):
        q = (zh, zb, zf, z2)[i]
        for t in range(AHC):
            y_last(ahslot(t), q)
        b = pl.ds(q * 4, 4)
        term = product(ah[b].reshape(256, 1024), o[b].reshape(256, 512))
        if i == 0:
            gd[...] = term
        else:
            gd[...] += term

    line(hslot(0), 1)
    z_first(ahslot(0))
    spread(ah_own[1], ahslot(1), own_c, (z_f, z_b))
    line(oslot, 1)
    line(hslot(0), 2)
    z_first(ahslot(1))
    spread(ai_in, aislot, own_c, (z_f, z_b))
    line(oslot, 2)
    z_second(ahslot(0))
    line(hslot(0), 3)
    to_sibling(o, os_sem, [oslot], local[3], 0)
    to_sibling(h, hs_sem, [hslot(t) for t in range(HC)], local[2], 0)
    line(oslot, 3)
    z_first(aislot)
    z_second(ahslot(1))
    to_sibling(o, os_sem, [oslot], local[3], 1)
    to_sibling(h, hs_sem, [hslot(t) for t in range(HC)], local[2], 1)
    z_second(aislot)
    to_sibling(o, os_sem, [oslot], local[3], 2)
    to_sibling(o, os_sem, [oslot], local[3], 3)
    to_sibling(h, hs_sem, [hslot(t) for t in range(HC)], local[2], 2)
    to_sibling(h, hs_sem, [hslot(t) for t in range(HC)], local[2], 3)
    local[1].wait()
    for q in range(4):
        arrived(o.at[pl.ds(q * 4, 4), 1 - core], os_sem.at[q])
    down_part(0)
    down_part(1)
    down_part(2)
    down_part(3)
    ctotal = jnp.zeros((8, 512), F32)
    for a in range(8):
        g = gd[a * 128 : a * 128 + 128, :]
        sq = g * g + EPS_SQUARE
        ctotal = ctotal + jnp.sum(sq.reshape(16, 8, 512), axis=0)
        lanes = sq[:, 0:128] + sq[:, 128:256] + sq[:, 256:384] + sq[:, 384:512]
        rpd[a : a + 1, :] = jnp.sum(jnp.transpose(lanes), axis=0, keepdims=True)
    csum = jnp.sum(ctotal, axis=0, keepdims=True)
    for j in range(4):
        cpd[j : j + 1, :] = csum[:, j * 128 : j * 128 + 128]

    start(rpd, rbufd, rd_sem, c, *in_col)
    start(cpd, cbufd, cd1_sem, on_x, *in_x)

    local[0].wait()
    for q in range(4):
        arrived(h.at[pl.ds(q * 4, 4), 1 - core], hs_sem.at[q])
    for q in (zh, zb, zf, z2):
        y_last(aislot, q)
    lhs = ai[...].reshape(1024, 256)

    def up_tile(n, carry):
        cols = pl.ds(pl.multiple_of(n * 512, 512), 512)
        gu[:, cols] = product(lhs, h[:, :, :, cols].reshape(1024, 512))
        return carry

    lax.fori_loop(0, 4, up_tile, 0)

    def up_squares(j, sums):
        cols = pl.ds(pl.multiple_of(j * 128, 128), 128)
        g = gu[:, cols]
        sq = g * g + EPS_SQUARE
        cpu[pl.ds(j, 1), :] = jnp.sum(sq, axis=0, keepdims=True)
        return sums + sq

    sums = lax.fori_loop(0, 16, up_squares, jnp.zeros((256, 128), F32))
    for a in range(2):
        rpu[a : a + 1, :] = jnp.sum(
            jnp.transpose(sums[a * 128 : a * 128 + 128]), axis=0, keepdims=True
        )


    start(cpu, cbufu, cu1_sem, on_x, *in_x)
    start(rpu, rbufu, ru_sem, c, *in_col)

    cpd2[...] = finish(cbufd, cd1_sem, 8)
    start(cpd2, cbufd2, cd2_sem, p, *in_line)
    cpu2[...] = finish(cbufu, cu1_sem, 8)
    start(cpu2, cbufu2, cu2_sem, p, *in_line)

    for k, (like, conds) in enumerate(sends):
        when(conds, lambda: pltpu.make_async_remote_copy(
            like(), like(), send_sem.at[k], loc_sem.at[0], sib, MESH).wait_send())
    for copy in local[4:]:
        copy.wait()

    keep, take = DECAY, 1.0 - DECAY
    cn = keep * csd[...] + take * (finish(cbufd2, cd2_sem, 4) / FF)
    cnd[...] = cn
    crd[...] = lax.rsqrt(cn)
    rn = keep * rsd[...] + take * (finish(rbufd, rd_sem, COLS) / D)
    rnd[...] = rn
    rroot = lax.rsqrt(rn)
    for a in range(8):
        rbd[a * 128 : a * 128 + 128, :] = jnp.transpose(
            jnp.broadcast_to(rroot[a : a + 1, :], (128, 128))
        )

    def down_raw(a, total):
        rows = pl.ds(pl.multiple_of(a * 128, 128), 128)
        for j in range(4):
            cols = slice(j * 128, j * 128 + 128)
            raw = gd[rows, cols] * rbd[rows, :] * crd[j : j + 1, :]
            gd[rows, cols] = raw
            total = total + jnp.sum((raw * raw).reshape(16, 8, 128), axis=0)
        return total

    td = lax.fori_loop(0, 8, down_raw, jnp.zeros((8, 128), F32))
    tp1[1:2, :] = jnp.sum(td, axis=0, keepdims=True)

    rn = keep * rsu[...] + take * (finish(rbufu, ru_sem, COLS) / FF)
    rnu[...] = rn
    rroot = lax.rsqrt(rn)
    for a in range(2):
        rbu[a * 128 : a * 128 + 128, :] = jnp.transpose(
            jnp.broadcast_to(rroot[a : a + 1, :], (128, 128))
        )
    cn = keep * csu[...] + take * (finish(cbufu2, cu2_sem, 4) / D)
    cnu[...] = cn
    cru[...] = lax.rsqrt(cn)

    def up_raw(j, total):
        cols = pl.ds(pl.multiple_of(j * 128, 128), 128)
        raw = gu[:, cols] * rbu[...] * cru[pl.ds(j, 1), :]
        gu[:, cols] = raw
        return total + jnp.sum((raw * raw).reshape(32, 8, 128), axis=0)

    tu = lax.fori_loop(0, 16, up_raw, jnp.zeros((8, 128), F32))
    tp1[0:1, :] = jnp.sum(tu, axis=0, keepdims=True)

    start(tp1, tbuf1, t1_sem, y * 8 + on_x, *in_plane)
    finish_sends(cbufu, cu1_sem, 8)
    finish_sends(rbufu, ru_sem, COLS)
    finish_sends(cbufu2, cu2_sem, 4)
    finish_sends(rbufd, rd_sem, COLS)
    finish_sends(cbufd, cd1_sem, 8)
    finish_sends(cbufd2, cd2_sem, 4)
    tp2[...] = finish(tbuf1, t1_sem, 32)
    start(tp2, tbuf2, t2_sem, zh * 4 + p, *in_z)
    finish_sends(tbuf1, t1_sem, 32)
    totals = finish(tbuf2, t2_sem, 16)
    rms = jnp.sqrt(jnp.sum(totals, axis=1, keepdims=True) / (float(D) * float(FF)))
    scale = 1.0 / jnp.maximum(CLIP_FLOOR, rms)

    def write(i, carry):
        rows = pl.ds(pl.multiple_of(i * 64, 64), 64)
        uu[rows, :] = (gu[rows, :] * scale[0:1, :]).astype(BF16)
        rows = pl.ds(pl.multiple_of(i * 256, 256), 256)
        ud[rows, :] = (gd[rows, :] * scale[1:2, :]).astype(BF16)
        return carry

    lax.fori_loop(0, 4, write, 0)
    finish_sends(tbuf2, t2_sem, 16)


def write_out(*refs):
    ins, outs, sem = refs[:6], refs[6:12], refs[12]
    copies = [
        pltpu.make_async_copy(a, b, sem.at[i]) for i, (a, b) in enumerate(zip(ins, outs))
    ]
    for copy in copies:
        copy.start()
    for copy in copies:
        copy.wait()


SHAPES = (
    ((256, 2048), BF16),
    ((2, 128), F32),
    ((16, 128), F32),
    ((1024, 512), BF16),
    ((8, 128), F32),
    ((4, 128), F32),
)


def on_device(ai, h, ah, o, rsu, csu, rsd, csd):
    dma = pltpu.SemaphoreType.DMA
    any_ = pl.BlockSpec(memory_space=pl.ANY)
    vmem = pl.BlockSpec(memory_space=pltpu.VMEM)
    f32 = lambda *shape: pltpu.VMEM(shape, F32)
    bf16 = lambda *shape: pltpu.VMEM(shape, BF16)
    res = pl.pallas_call(
        kernel,
        out_shape=tuple(pltpu.VMEM(shape, dtype) for shape, dtype in SHAPES),
        in_specs=[any_] * 8,
        out_specs=[vmem] * 6,
        scratch_shapes=[
            bf16(NB, 64, 256), bf16(NB, 64, 1024), bf16(NB, 2, 32, 2048), bf16(NB, 2, 32, 512),
            f32(256, 2048), f32(1024, 512), f32(256, 128), f32(1024, 128),
            f32(2, 128), f32(16, 128), f32(8, 128), f32(4, 128), f32(16, 128), f32(4, 128),
            f32(2, 128), f32(16, 128), f32(16, 128), f32(8, 128), f32(4, 128), f32(4, 128),
            f32(COLS, 2, 128), f32(8, 16, 128), f32(4, 16, 128), f32(COLS, 8, 128), f32(8, 4, 128), f32(4, 4, 128),
            f32(2, 128), f32(32, 2, 128), f32(2, 128), f32(16, 2, 128),
            dma((NB,)), dma((NB, AHC)), dma((NB, HC)), dma((NB,)), dma((4,)), dma((4,)),
            dma((NSEND,)), dma((8,)),
            *[dma((2,))] * 6,
            *[dma((2,))] * 2,
        ],
        compiler_params=pltpu.CompilerParams(
            collective_id=0, has_side_effects=True, vmem_limit_bytes=VMEM_MB * 1024 * 1024
        ),
        cost_estimate=pl.CostEstimate(
            flops=2 * 2 * 1024 * 256 * 2048, bytes_accessed=3 << 20, transcendentals=0
        ),
    )(ai, h, ah, o, rsu.reshape(2, 128), csu.reshape(16, 128), rsd.reshape(8, 128), csd.reshape(4, 128))
    uu, rnu, cnu, ud, rnd, cnd = pl.pallas_call(
        write_out,
        out_shape=tuple(pltpu.HBM(shape, dtype) for shape, dtype in SHAPES),
        in_specs=[vmem] * 6,
        out_specs=[pl.BlockSpec(memory_space=pltpu.HBM)] * 6,
        scratch_shapes=[dma((6,))],
        compiler_params=pltpu.CompilerParams(has_side_effects=True),
    )(*[pltpu.with_memory_space_constraint(t, pltpu.VMEM) for t in res])
    return (uu, rnu.reshape(256), cnu.reshape(2048), ud, rnd.reshape(1024), cnd.reshape(512))


def solution(mesh):
    in_specs = (
        P("col", "row"),
        P("row", "col"),
        P("col", "row"),
        P("row", "col"),
        P("row"),
        P("col"),
        P("row"),
        P("col"),
    )
    out_specs = (P("row", "col"), P("row"), P("col"), P("row", "col"), P("row"), P("col"))
    return jax.shard_map(
        on_device, mesh=mesh, in_specs=in_specs, out_specs=out_specs, check_vma=False
    )
```

```python
import jax
import jax.numpy as jnp
from jax import lax
from jax.experimental import pallas as pl
from jax.experimental.pallas import tpu as pltpu
from jax.sharding import PartitionSpec as P

D = 8192
FF = 32768
DECAY = 1.0 - 10.0 ** (-0.8)
EPS_SQUARE = 1e-30
CLIP_FLOOR = 0.1

NB = 16
ROWS = 32
COLS = 16
HC = 1
AHC = 2
F32 = jnp.float32
BF16 = jnp.bfloat16
MESH = pl.DeviceIdType.MESH
NSEND = 240
VMEM_MB = 57


def mod(a, n):
    return lax.rem(a + n, n)


def kernel(
    ai_in, h_in, ah_in, o_in, rsu_in, csu_in, rsd_in, csd_in,
    uu, rnu, cnu, ud, rnd, cnd,
    ai, ah, h, o, gu, gd, rbu, rbd, rsu, csu, rsd, csd, cru, crd,
    rpu, cpu, cpu2, rpd, cpd, cpd2, rbufu, cbufu, cbufu2, rbufd, cbufd, cbufd2, tp1, tbuf1, tp2, tbuf2,
    ai_sem, ah_sem, h_sem, o_sem, hs_sem, os_sem, send_sem, loc_sem,
    rd_sem, cd1_sem, cd2_sem, ru_sem, cu1_sem, cu2_sem, t1_sem, t2_sem,
):
    r = lax.axis_index("row")
    c = lax.axis_index("col")
    core = lax.rem(r, 2)
    x = lax.rem(r // 2, 4)
    p = r // 8
    y = lax.rem(c, 4)
    zh = c // 4
    s = 1 - 2 * core

    def row_at(zl_, x_, core_):
        return (zl_ * 8 + x_ * 2 + core_, c)

    def col_at(zh_, y_):
        return (r, zh_ * 4 + y_)

    zf, zb, z2 = mod(zh + s, 4), mod(zh - s, 4), mod(zh + 2, 4)
    xs = [row_at(p, mod(x + i, 4), core) for i in (2, 1, 3)]
    ys = [col_at(zh, mod(y + i, 4)) for i in (2, 1, 3)]
    z_f, z_b = col_at(zf, y), col_at(zb, y)
    l_f, l_b = row_at(mod(p + 1, 4), x, core), row_at(mod(p - 1, 4), x, core)
    sib = row_at(p, x, 1 - core)

    barrier = pltpu.get_barrier_semaphore()
    for dev in (z_f, z_b, l_f, l_b, *xs, *ys, sib):
        pl.semaphore_signal(barrier, inc=1, device_id=dev, device_id_type=MESH)
    pl.semaphore_wait(barrier, 11)

    sends = []

    def send(src, dst, recv, like, dev, conds=()):
        k = len(sends)
        pltpu.make_async_remote_copy(src, dst, send_sem.at[k], recv, dev, MESH).start()
        sends.append((like, conds))

    def when(conds, f):
        if not conds:
            f()
        else:
            pl.when(conds[0])(lambda: when(conds[1:], f))

    def arrived(dst, recv, like=None):
        pltpu.make_async_remote_copy(dst, dst, send_sem.at[0], recv, sib, MESH).wait_recv()

    HT = 32 // HC

    def hslot(t):
        part = pl.ds(t * HT, HT)

        def slot(b):
            return h.at[b, core, part], h_sem.at[b, t], lambda: h.at[0, 0, part]

        return slot

    def oslot(b):
        return o.at[b, core], o_sem.at[b], lambda: o.at[0, 0]

    def aislot(b):
        return ai.at[b], ai_sem.at[b], lambda: ai.at[0]

    AHT = 64 // AHC

    def ahslot(t):
        part = pl.ds(t * AHT, AHT)

        def slot(b):
            return ah.at[b, part], ah_sem.at[b, t], lambda: ah.at[0, part]

        return slot

    not_last, not_first = p < 3, p > 0
    own_r, own_c = p * 4 + x, c
    h_own = [h_in.at[pl.ds(t * HT, HT)] for t in range(HC)]
    ah_own = [ah_in.at[pl.ds(t * AHT, AHT)] for t in range(AHC)]

    def line_own(src, slot):
        @pl.when(not_last)
        def _():
            send(src, *slot(own_r), l_f, (not_last,))

        @pl.when(not_first)
        def _():
            send(src, *slot(own_r), l_b, (not_first,))

    def spread(src, slot, b, devs, conds=()):
        for dev in devs:
            send(src, *slot(b), dev, conds)

    line_own(h_own[0], hslot(0))
    spread(ai_in, aislot, own_c, (z_f, z_b))
    spread(ah_own[0], ahslot(0), own_c, (z_f, z_b))
    line_own(o_in, oslot)
    for t in range(HC):
        spread(h_own[t], hslot(t), own_r, xs)
    spread(ai_in, aislot, own_c, ys)
    for t in range(AHC):
        spread(ah_own[t], ahslot(t), own_c, ys)
    spread(o_in, oslot, own_r, xs)

    local = [
        pltpu.make_async_copy(ai_in, ai.at[own_c], loc_sem.at[0]),
        pltpu.make_async_copy(ah_in, ah.at[own_c], loc_sem.at[1]),
        pltpu.make_async_copy(h_in, h.at[own_r, core], loc_sem.at[2]),
        pltpu.make_async_copy(o_in, o.at[own_r, core], loc_sem.at[3]),
        pltpu.make_async_copy(rsu_in, rsu, loc_sem.at[4]),
        pltpu.make_async_copy(rsd_in, rsd, loc_sem.at[5]),
        pltpu.make_async_copy(csu_in, csu, loc_sem.at[6]),
        pltpu.make_async_copy(csd_in, csd, loc_sem.at[7]),
    ]
    for copy in local:
        copy.start()

    def line(slot, d):
        left, right = p >= d, p + d <= 3

        def one(b, further, dev, conds):
            arrived(*slot(b))
            if d < 3:
                @pl.when(further)
                def _():
                    send(slot(b)[0], *slot(b), dev, conds + (further,))
            spread(slot(b)[0], slot, b, xs, conds)

        pl.when(left)(lambda: one((p - d) * 4 + x, not_last, l_f, (left,)))
        pl.when(right)(lambda: one((p + d) * 4 + x, not_first, l_b, (right,)))

    def z_one(slot, zz, onward=False):
        b = zz * 4 + y
        arrived(*slot(b))
        if onward:
            send(slot(b)[0], *slot(b), z_f)
        spread(slot(b)[0], slot, b, ys)

    def z_first(slot):
        z_one(slot, zb, True)
        z_one(slot, zf)

    def z_second(slot):
        z_one(slot, z2)

    def to_sibling(buf, sem, slots, mine, d):
        def one(q, conds):
            for i in (1, 3, 2):
                for slot in slots:
                    arrived(*slot(q * 4 + mod(x + i, 4)))
            part = buf.at[pl.ds(q * 4, 4), core]
            send(part, part, sem.at[q], lambda: buf.at[pl.ds(0, 4), 0], sib, conds)

        if d == 0:
            mine.wait()
            one(p, ())
        else:
            left, right = p >= d, p + d <= 3
            pl.when(left)(lambda: one(p - d, (left,)))
            pl.when(right)(lambda: one(p + d, (right,)))

    def y_last(slot, q):
        for i in (1, 3, 2):
            arrived(*slot(q * 4 + mod(y + i, 4)))

    def product(a, b):
        return lax.dot_general(a, b, (((0,), (0,)), ((), ())), preferred_element_type=F32)


    def start(part, buf, sem, me, *groups):
        for first, last, where in groups:

            def one(k, carry, where=where):
                pltpu.make_async_remote_copy(
                    part, buf.at[me], sem.at[1], sem.at[0], where(k), MESH
                ).start()
                return carry

            lax.fori_loop(first, last, one, 0)
        buf[me] = part[...]

    def finish(buf, sem, n):
        others = buf.at[pl.ds(0, n - 1)]
        pltpu.make_async_remote_copy(others, others, sem.at[1], sem.at[0], sib, MESH).wait_recv()
        return jnp.sum(buf[...], axis=0)

    def finish_sends(buf, sem, n):
        others = buf.at[pl.ds(0, n - 1)]
        pltpu.make_async_remote_copy(others, others, sem.at[1], sem.at[0], sib, MESH).wait_send()

    on_x = x * 2 + core
    in_x = ((1, 8, lambda k: (p * 8 + lax.rem(on_x + k, 8), c)),)
    in_line = tuple((d, d + 1, lambda k: (lax.rem(p + k, 4) * 8 + on_x, c)) for d in (2, 1, 3))

    def around(d, first, last, group, base):
        at = group(d)
        return (first, last, lambda k: base(at, k))

    def col_of(d):
        return around(d, 1 if d == 0 else 0, 4, lambda d: mod(zh + d, 4) * 4, lambda at, k: (r, at + lax.rem(y + k, 4)))

    def plane_of(d):
        return around(d, 1 if d == 0 else 0, 8, lambda d: zh * 4 + mod(y + d, 4), lambda at, k: (p * 8 + lax.rem(on_x + k, 8), at))

    def z_of(d):
        return around(d, 1 if d == 0 else 0, 4, lambda d: mod(zh + d, 4) * 4 + y, lambda at, k: (lax.rem(p + k, 4) * 8 + on_x, at))

    in_col = [col_of(d) for d in (2, 1, 3, 0)]
    in_plane = [plane_of(d) for d in (2, 1, 3, 0)]
    in_z = [z_of(d) for d in (2, 1, 3, 0)]

    def down_part(i):
        q = (zh, zb, zf, z2)[i]
        for t in range(AHC):
            y_last(ahslot(t), q)
        b = pl.ds(q * 4, 4)
        term = product(ah[b].reshape(256, 1024), o[b].reshape(256, 512))
        if i == 0:
            gd[...] = term
        else:
            gd[...] += term

    line(hslot(0), 1)
    z_first(aislot)
    z_first(ahslot(0))
    spread(ah_own[1], ahslot(1), own_c, (z_f, z_b))
    line(oslot, 1)
    line(hslot(0), 2)
    z_second(aislot)
    z_first(ahslot(1))
    line(oslot, 2)
    z_second(ahslot(0))
    line(hslot(0), 3)
    to_sibling(o, os_sem, [oslot], local[3], 0)
    to_sibling(h, hs_sem, [hslot(t) for t in range(HC)], local[2], 0)
    line(oslot, 3)
    z_second(ahslot(1))
    to_sibling(o, os_sem, [oslot], local[3], 1)
    to_sibling(h, hs_sem, [hslot(t) for t in range(HC)], local[2], 1)
    to_sibling(o, os_sem, [oslot], local[3], 2)
    to_sibling(o, os_sem, [oslot], local[3], 3)
    to_sibling(h, hs_sem, [hslot(t) for t in range(HC)], local[2], 2)
    to_sibling(h, hs_sem, [hslot(t) for t in range(HC)], local[2], 3)

    local[0].wait()
    for q in range(4):
        arrived(h.at[pl.ds(q * 4, 4), 1 - core], hs_sem.at[q])
    for q in (zh, zb, zf, z2):
        y_last(aislot, q)
    lhs = ai[...].reshape(1024, 256)

    def up_tile(n, carry):
        cols = pl.ds(pl.multiple_of(n * 512, 512), 512)
        gu[:, cols] = product(lhs, h[:, :, :, cols].reshape(1024, 512))
        return carry

    lax.fori_loop(0, 4, up_tile, 0)

    def up_squares(j, sums):
        cols = pl.ds(pl.multiple_of(j * 128, 128), 128)
        g = gu[:, cols]
        sq = g * g + EPS_SQUARE
        cpu[pl.ds(j, 1), :] = jnp.sum(sq, axis=0, keepdims=True)
        return sums + sq

    sums = lax.fori_loop(0, 16, up_squares, jnp.zeros((256, 128), F32))
    for a in range(2):
        rpu[a : a + 1, :] = jnp.sum(
            jnp.transpose(sums[a * 128 : a * 128 + 128]), axis=0, keepdims=True
        )


    start(cpu, cbufu, cu1_sem, on_x, *in_x)
    start(rpu, rbufu, ru_sem, c, *in_col)
    local[1].wait()
    for q in range(4):
        arrived(o.at[pl.ds(q * 4, 4), 1 - core], os_sem.at[q])
    down_part(0)
    down_part(1)
    down_part(2)
    down_part(3)
    ctotal = jnp.zeros((8, 512), F32)
    for a in range(8):
        g = gd[a * 128 : a * 128 + 128, :]
        sq = g * g + EPS_SQUARE
        ctotal = ctotal + jnp.sum(sq.reshape(16, 8, 512), axis=0)
        lanes = sq[:, 0:128] + sq[:, 128:256] + sq[:, 256:384] + sq[:, 384:512]
        rpd[a : a + 1, :] = jnp.sum(jnp.transpose(lanes), axis=0, keepdims=True)
    csum = jnp.sum(ctotal, axis=0, keepdims=True)
    for j in range(4):
        cpd[j : j + 1, :] = csum[:, j * 128 : j * 128 + 128]

    start(rpd, rbufd, rd_sem, c, *in_col)
    start(cpd, cbufd, cd1_sem, on_x, *in_x)

    cpd2[...] = finish(cbufd, cd1_sem, 8)
    start(cpd2, cbufd2, cd2_sem, p, *in_line)
    cpu2[...] = finish(cbufu, cu1_sem, 8)
    start(cpu2, cbufu2, cu2_sem, p, *in_line)

    for k, (like, conds) in enumerate(sends):
        when(conds, lambda: pltpu.make_async_remote_copy(
            like(), like(), send_sem.at[k], loc_sem.at[0], sib, MESH).wait_send())
    for copy in local[4:]:
        copy.wait()

    keep, take = DECAY, 1.0 - DECAY
    cn = keep * csd[...] + take * (finish(cbufd2, cd2_sem, 4) / FF)
    cnd[...] = cn
    crd[...] = lax.rsqrt(cn)
    rn = keep * rsd[...] + take * (finish(rbufd, rd_sem, COLS) / D)
    rnd[...] = rn
    rroot = lax.rsqrt(rn)
    for a in range(8):
        rbd[a * 128 : a * 128 + 128, :] = jnp.transpose(
            jnp.broadcast_to(rroot[a : a + 1, :], (128, 128))
        )

    def down_raw(a, total):
        rows = pl.ds(pl.multiple_of(a * 128, 128), 128)
        for j in range(4):
            cols = slice(j * 128, j * 128 + 128)
            raw = gd[rows, cols] * rbd[rows, :] * crd[j : j + 1, :]
            gd[rows, cols] = raw
            total = total + jnp.sum((raw * raw).reshape(16, 8, 128), axis=0)
        return total

    td = lax.fori_loop(0, 8, down_raw, jnp.zeros((8, 128), F32))
    tp1[1:2, :] = jnp.sum(td, axis=0, keepdims=True)

    rn = keep * rsu[...] + take * (finish(rbufu, ru_sem, COLS) / FF)
    rnu[...] = rn
    rroot = lax.rsqrt(rn)
    for a in range(2):
        rbu[a * 128 : a * 128 + 128, :] = jnp.transpose(
            jnp.broadcast_to(rroot[a : a + 1, :], (128, 128))
        )
    cn = keep * csu[...] + take * (finish(cbufu2, cu2_sem, 4) / D)
    cnu[...] = cn
    cru[...] = lax.rsqrt(cn)

    def up_raw(j, total):
        cols = pl.ds(pl.multiple_of(j * 128, 128), 128)
        raw = gu[:, cols] * rbu[...] * cru[pl.ds(j, 1), :]
        gu[:, cols] = raw
        return total + jnp.sum((raw * raw).reshape(32, 8, 128), axis=0)

    tu = lax.fori_loop(0, 16, up_raw, jnp.zeros((8, 128), F32))
    tp1[0:1, :] = jnp.sum(tu, axis=0, keepdims=True)

    start(tp1, tbuf1, t1_sem, y * 8 + on_x, *in_plane)
    finish_sends(cbufu, cu1_sem, 8)
    finish_sends(rbufu, ru_sem, COLS)
    finish_sends(cbufu2, cu2_sem, 4)
    finish_sends(rbufd, rd_sem, COLS)
    finish_sends(cbufd, cd1_sem, 8)
    finish_sends(cbufd2, cd2_sem, 4)
    tp2[...] = finish(tbuf1, t1_sem, 32)
    start(tp2, tbuf2, t2_sem, zh * 4 + p, *in_z)
    finish_sends(tbuf1, t1_sem, 32)
    totals = finish(tbuf2, t2_sem, 16)
    rms = jnp.sqrt(jnp.sum(totals, axis=1, keepdims=True) / (float(D) * float(FF)))
    scale = 1.0 / jnp.maximum(CLIP_FLOOR, rms)

    def write(i, carry):
        rows = pl.ds(pl.multiple_of(i * 64, 64), 64)
        uu[rows, :] = (gu[rows, :] * scale[0:1, :]).astype(BF16)
        rows = pl.ds(pl.multiple_of(i * 256, 256), 256)
        ud[rows, :] = (gd[rows, :] * scale[1:2, :]).astype(BF16)
        return carry

    lax.fori_loop(0, 4, write, 0)
    finish_sends(tbuf2, t2_sem, 16)


def write_out(*refs):
    ins, outs, sem = refs[:6], refs[6:12], refs[12]
    copies = [
        pltpu.make_async_copy(a, b, sem.at[i]) for i, (a, b) in enumerate(zip(ins, outs))
    ]
    for copy in copies:
        copy.start()
    for copy in copies:
        copy.wait()


SHAPES = (
    ((256, 2048), BF16),
    ((2, 128), F32),
    ((16, 128), F32),
    ((1024, 512), BF16),
    ((8, 128), F32),
    ((4, 128), F32),
)


def on_device(ai, h, ah, o, rsu, csu, rsd, csd):
    dma = pltpu.SemaphoreType.DMA
    any_ = pl.BlockSpec(memory_space=pl.ANY)
    vmem = pl.BlockSpec(memory_space=pltpu.VMEM)
    f32 = lambda *shape: pltpu.VMEM(shape, F32)
    bf16 = lambda *shape: pltpu.VMEM(shape, BF16)
    res = pl.pallas_call(
        kernel,
        out_shape=tuple(pltpu.VMEM(shape, dtype) for shape, dtype in SHAPES),
        in_specs=[any_] * 8,
        out_specs=[vmem] * 6,
        scratch_shapes=[
            bf16(NB, 64, 256), bf16(NB, 64, 1024), bf16(NB, 2, 32, 2048), bf16(NB, 2, 32, 512),
            f32(256, 2048), f32(1024, 512), f32(256, 128), f32(1024, 128),
            f32(2, 128), f32(16, 128), f32(8, 128), f32(4, 128), f32(16, 128), f32(4, 128),
            f32(2, 128), f32(16, 128), f32(16, 128), f32(8, 128), f32(4, 128), f32(4, 128),
            f32(COLS, 2, 128), f32(8, 16, 128), f32(4, 16, 128), f32(COLS, 8, 128), f32(8, 4, 128), f32(4, 4, 128),
            f32(2, 128), f32(32, 2, 128), f32(2, 128), f32(16, 2, 128),
            dma((NB,)), dma((NB, AHC)), dma((NB, HC)), dma((NB,)), dma((4,)), dma((4,)),
            dma((NSEND,)), dma((8,)),
            *[dma((2,))] * 6,
            *[dma((2,))] * 2,
        ],
        compiler_params=pltpu.CompilerParams(
            collective_id=0, has_side_effects=True, vmem_limit_bytes=VMEM_MB * 1024 * 1024
        ),
        cost_estimate=pl.CostEstimate(
            flops=2 * 2 * 1024 * 256 * 2048, bytes_accessed=3 << 20, transcendentals=0
        ),
    )(ai, h, ah, o, rsu.reshape(2, 128), csu.reshape(16, 128), rsd.reshape(8, 128), csd.reshape(4, 128))
    uu, rnu, cnu, ud, rnd, cnd = pl.pallas_call(
        write_out,
        out_shape=tuple(pltpu.HBM(shape, dtype) for shape, dtype in SHAPES),
        in_specs=[vmem] * 6,
        out_specs=[pl.BlockSpec(memory_space=pltpu.HBM)] * 6,
        scratch_shapes=[dma((6,))],
        compiler_params=pltpu.CompilerParams(has_side_effects=True),
    )(*[pltpu.with_memory_space_constraint(t, pltpu.VMEM) for t in res])
    return (uu, rnu.reshape(256), cnu.reshape(2048), ud, rnd.reshape(1024), cnd.reshape(512))


def solution(mesh):
    in_specs = (
        P("col", "row"),
        P("row", "col"),
        P("col", "row"),
        P("row", "col"),
        P("row"),
        P("col"),
        P("row"),
        P("col"),
    )
    out_specs = (P("row", "col"), P("row"), P("col"), P("row", "col"), P("row"), P("col"))
    return jax.shard_map(
        on_device, mesh=mesh, in_specs=in_specs, out_specs=out_specs, check_vma=False
    )
```
